32 devices in a mesh: dp: 8 (over z, x), seq: 4 (over y, core).
Axes of the slice: x: 2, y: 2, z: 4, core: 2. Of those that a mesh axis runs over, the one named last changes fastest.
Arguments:
- hidden_in: bfloat16 [16, 2048, 768], P('dp', 'seq'), may hold values from -6 to 6
- cotangent: bfloat16 [16, 2048, 768], P('dp', 'seq'), may hold values from -6 to 6
- lengths: int32 [16], P('dp'), may hold values from 128 to 2048, as said below
- qkv_weight: bfloat16 [768, 2304], P('dp'), may hold values from -0.21875 to 0.21875
- q_bias: bfloat16 [768], P('dp'), may hold values from -3 to 3
- v_bias: bfloat16 [768], P('dp'), may hold values from -0.4375 to 0.4375
- out_weight: bfloat16 [768, 768], P('dp'), may hold values from -6 to 6
- out_bias: bfloat16 [768], P('dp'), may hold values from -3 to 3
- norm1_gain: bfloat16 [768], P('dp'), may hold values from 0.099609375 to 1.8984375
- norm1_shift: bfloat16 [768], P('dp'), may hold values from -3 to 3
- up_weight: bfloat16 [768, 3072], P('dp'), may hold values from -0.21875 to 0.21875
- up_bias: bfloat16 [3072], P('dp'), may hold values from -3 to 3
- down_weight: bfloat16 [3072, 768], P('dp'), may hold values from -0.109375 to 0.109375
- down_bias: bfloat16 [768], P('dp'), may hold values from -3 to 3
- norm2_gain: bfloat16 [768], P('dp'), may hold values from 0.099609375 to 1.8984375
- norm2_shift: bfloat16 [768], P('dp'), may hold values from -3 to 3
Outputs:
- out_hidden: bfloat16 [16, 2048, 768], P('dp', 'seq')
- grad_hidden: bfloat16 [16, 2048, 768], P('dp', 'seq')
- grad_qkv_weight: float32 [768, 2304], P('dp')
- grad_q_bias: float32 [768], P('dp')
- grad_v_bias: float32 [768], P('dp')
- grad_out_weight: float32 [768, 768], P('dp')
- grad_out_bias: float32 [768], P('dp')
- grad_norm1_gain: float32 [768], P('dp')
- grad_norm1_shift: float32 [768], P('dp')
- grad_up_weight: float32 [768, 3072], P('dp')
- grad_up_bias: float32 [3072], P('dp')
- grad_down_weight: float32 [3072, 768], P('dp')
- grad_down_bias: float32 [768], P('dp')
- grad_norm2_gain: float32 [768], P('dp')
- grad_norm2_shift: float32 [768], P('dp')
The draws below stay inside these ranges and needn't reach their ends.
Inputs may be any that keep to these rules, and one draw needn't show every extreme that they name: `lengths`: of the sequences 0 to 1, 2 to 3 and so on, one in each run has length 2048.
All inputs are finite; a program needn't handle non-finite values.
Results may differ from the reference program's by a relative error of at most 0.017.
The reference program's roundings to bfloat16 on the way count: a program that leaves them out, or rounds other values in their place, can miss the bound.
Values may be sent and summed in bfloat16 or wider, within the bound.
A program may use at most 192 MiB of HBM per device.

```python
import jax
import jax.numpy as jnp
from jax import lax

D = 768
H = 12
HD = 64
FF = 3072
SEQ_LEN = 2048
SEQ_GROUP = 2
SEQS = 16


def draw_lengths(key, part):
    key = jax.random.fold_in(key, 7)
    first_key, second_key = jax.random.split(key)
    sampled = jax.random.randint(first_key, (SEQS,), SEQ_LEN // 16, SEQ_LEN + 1)
    chosen = jax.random.randint(second_key, (SEQS // SEQ_GROUP,), 0, SEQ_GROUP)
    position = jnp.arange(SEQS) % SEQ_GROUP
    longest = position == jnp.repeat(chosen, SEQ_GROUP)
    return jnp.where(longest, SEQ_LEN, sampled).astype(jnp.int32)


def spiked(drawn, stream_key, source, target, shards_of, factor):
    def block_of(dim):
        return (jnp.arange(drawn.shape[dim]) // (drawn.shape[dim] // shards_of)).reshape((-1,) + (1,) * (drawn.ndim - 1 - dim))

    near = jax.random.permutation(stream_key, shards_of)[block_of(target)]
    other_side = (block_of(target) + shards_of // 2) % shards_of
    return jnp.where((block_of(source) == near) | (block_of(source) == other_side), factor * drawn, drawn)


def block_scale(key, dims, cuts, low, top_value):
    loudness, own = 1.0, jax.random.fold_in(key, 6)
    for dim, parts in cuts:
        heights = jnp.exp(jax.random.uniform(jax.random.fold_in(own, dim), (parts,), jnp.float32, low / len(cuts), top_value / len(cuts)))
        loudness = loudness * jnp.repeat(heights, dims[dim] // parts).reshape([-1 if axis == dim else 1 for axis in range(len(dims))])
    return loudness


def gaussian(stream_key, dims, width, limit, cuts=(), dtype=jnp.bfloat16):
    gain = block_scale(stream_key, dims, cuts, -0.22, 0.18) if cuts else 1.0
    values = jax.random.normal(stream_key, dims, jnp.float32) * width * gain
    return jnp.minimum(jnp.maximum(values, -limit), limit).astype(dtype)


def gaussian_with(stream_key, extent, width, bound, cuts, heavy, held_as=jnp.bfloat16):
    array = width * jax.random.normal(stream_key, extent, jnp.float32)
    if cuts:
        array = array * block_scale(stream_key, extent, cuts, -0.22, 0.18)
    return jnp.clip(spiked(array, jax.random.fold_in(stream_key, 3), *heavy), -bound, bound).astype(held_as)


def setup_inputs(seed: int = 0) -> dict:
    keys = jax.random.split(jax.random.key(seed), 17)
    hidden_in = gaussian_with(keys[0], (SEQS, SEQ_LEN, D), 1.0, 6.0, ((0, 8), (1, 4)), (0, 2, 8, 2.0))
    cotangent = gaussian_with(keys[1], (SEQS, SEQ_LEN, D), 1.0, 6.0, ((0, 8), (1, 4)), (0, 2, 8, 2.0))
    lengths = draw_lengths(jax.random.fold_in(keys[16], 71), 0)
    qkv_weight = gaussian(keys[3], (D, 3 * D), D ** -0.5, 0.21875, ((0, 8),))
    q_bias = gaussian(keys[4], (D,), 0.5, 3.0, ((0, 8),))
    v_bias = gaussian(keys[5], (D,), 0.03, 0.4375, ((0, 8),))
    out_weight = gaussian(keys[6], (D, D), (2 * D // SEQ_LEN + 1) ** -0.5, 6.0, ((0, 8),))
    out_bias = gaussian(keys[7], (D,), 0.3, 3.0, ((0, 8),))
    norm1_gain = jnp.clip(1.0 + 0.18 * jax.random.normal(keys[8], (D,), jnp.float32), 0.099609375, 1.8984375).astype(jnp.bfloat16)
    norm1_shift = gaussian(keys[9], (D,), 0.3, 3.0, ((0, 8),))
    up_weight = gaussian(keys[10], (D, FF), D ** -0.5, 0.21875, ((0, 8),))
    up_bias = gaussian(keys[11], (FF,), 0.5, 3.0, ((0, 8),))
    down_weight = gaussian(keys[12], (FF, D), FF ** -0.5, 0.109375, ((0, 8),))
    down_bias = gaussian(keys[13], (D,), 0.3, 3.0, ((0, 8),))
    norm2_gain = jnp.clip(1.0 + 0.18 * jax.random.normal(keys[14], (D,), jnp.float32), 0.099609375, 1.8984375).astype(jnp.bfloat16)
    norm2_shift = gaussian(keys[15], (D,), 0.3, 3.0, ((0, 8),))
    return dict(hidden_in=hidden_in, cotangent=cotangent, lengths=lengths, qkv_weight=qkv_weight, q_bias=q_bias, v_bias=v_bias, out_weight=out_weight, out_bias=out_bias, norm1_gain=norm1_gain, norm1_shift=norm1_shift, up_weight=up_weight, up_bias=up_bias, down_weight=down_weight, down_bias=down_bias, norm2_gain=norm2_gain, norm2_shift=norm2_shift)


@jax.custom_vjp
def low(v):
    return lax.optimization_barrier(v.astype(jnp.bfloat16)).astype(jnp.float32)

@jax.custom_vjp
def low_back(v):
    return v

def low_keep(v):
    return (low(v), None)

def low_pass(kept, grad):
    return (grad,)

def back_keep(v):
    return (v, None)

def back_low(kept, grad):
    return (low(grad),)
low.defvjp(low_keep, low_pass)
low_back.defvjp(back_keep, back_low)
epsilon = 1e-06
highest = lax.Precision.HIGHEST

def norm_rows(values_in, gain_vec, shift_vec):
    centered = values_in - lax.optimization_barrier(jnp.mean(values_in, axis=-1, keepdims=True))
    variance = lax.optimization_barrier(jnp.mean(centered * centered, axis=-1, keepdims=True))
    return centered * lax.rsqrt(variance + epsilon) * gain_vec + shift_vec

def matmul(first_op, second_op):
    return jnp.dot(first_op, second_op, precision=highest, preferred_element_type=jnp.float32)

def attend(inputs_one):
    queries, keys_all, values_all, length = inputs_one
    scores = jnp.einsum('qhd,khd->hqk', queries, keys_all, precision=highest) * HD ** (-0.5)
    scores = low_back(scores)
    key_valid = jnp.arange(SEQ_LEN) < length
    scores = jnp.where(key_valid[None, None, :], scores, -1e+30)
    weights_low = low(jax.nn.softmax(scores, axis=-1))
    return jnp.einsum('hqk,khd->qhd', weights_low, values_all, precision=highest)

def layer(hidden, lengths, qkv_weight, q_bias, v_bias, out_weight, out_bias, norm1_gain, norm1_shift, up_weight, up_bias, down_weight, down_bias, norm2_gain, norm2_shift):
    token_rows = hidden.reshape(SEQS * SEQ_LEN, D)
    bias_all = jnp.concatenate([q_bias, jnp.zeros_like(q_bias), v_bias])
    projected = low_back(low(matmul(token_rows, qkv_weight) + bias_all))
    by_heads = projected.reshape(SEQS, SEQ_LEN, 3, H, HD)
    context = lax.map(jax.checkpoint(attend), (by_heads[:, :, 0], by_heads[:, :, 1], by_heads[:, :, 2], lengths))
    context = low_back(low(context.reshape(SEQS * SEQ_LEN, D)))
    attended = low_back(matmul(context, out_weight) + out_bias)
    first_norm = norm_rows(token_rows + attended, norm1_gain, norm1_shift)
    pre_act = low_back(matmul(low(first_norm), up_weight) + up_bias)
    activated = low(jax.nn.gelu(pre_act, approximate=False))
    branch = low_back(matmul(activated, down_weight) + down_bias)
    result = norm_rows(first_norm + branch, norm2_gain, norm2_shift)
    return result.reshape(SEQS, SEQ_LEN, D)

def reference(hidden_in, cotangent, lengths, qkv_weight, q_bias, v_bias, out_weight, out_bias, norm1_gain, norm1_shift, up_weight, up_bias, down_weight, down_bias, norm2_gain, norm2_shift):

    def forward(hidden, w_qkv, b_query, b_value, w_out, b_out, g_one, s_one, w_up, b_up, w_down, b_down, g_two, s_two):
        return layer(hidden, lengths, w_qkv, b_query, b_value, w_out, b_out, g_one, s_one, w_up, b_up, w_down, b_down, g_two, s_two)
    output, pullback = jax.vjp(forward, hidden_in.astype(jnp.float32), qkv_weight.astype(jnp.float32), q_bias.astype(jnp.float32), v_bias.astype(jnp.float32), out_weight.astype(jnp.float32), out_bias.astype(jnp.float32), norm1_gain.astype(jnp.float32), norm1_shift.astype(jnp.float32), up_weight.astype(jnp.float32), up_bias.astype(jnp.float32), down_weight.astype(jnp.float32), down_bias.astype(jnp.float32), norm2_gain.astype(jnp.float32), norm2_shift.astype(jnp.float32))
    g_hidden, g_qkv, g_qbias, g_vbias, g_out, g_obias, g_gone, g_sone, g_up, g_ubias, g_down, g_dbias, g_gtwo, g_stwo = pullback(cotangent.astype(jnp.float32))
    return (output.astype(jnp.bfloat16), g_hidden.astype(jnp.bfloat16), g_qkv, g_qbias, g_vbias, g_out, g_obias, g_gone, g_sone, g_up, g_ubias, g_down, g_dbias, g_gtwo, g_stwo)
```

```python
import functools

import jax
import jax.numpy as jnp
from jax import lax
from jax.experimental import pallas as pl
from jax.experimental.pallas import tpu as pltpu
from jax.sharding import PartitionSpec as P

HD = 64


epsilon = 1e-06


def norm_rows(values_in, gain_vec, shift_vec):
    centered = values_in - jnp.mean(values_in, axis=-1, keepdims=True)
    variance = jnp.mean(centered * centered, axis=-1, keepdims=True)
    return centered * lax.rsqrt(variance + epsilon) * gain_vec + shift_vec


def gelu_exact(values_in):
    return jax.nn.gelu(values_in, approximate=False)


def matmul(first_op, second_op):
    return jnp.dot(first_op, second_op, preferred_element_type=jnp.float32)


def inner_rows(first_op, second_op):
    return lax.dot_general(
        first_op, second_op, (((0,), (0,)), ((), ())), preferred_element_type=jnp.float32
    )


def inner_cols(first_op, second_op):
    return lax.dot_general(
        first_op, second_op, (((1,), (1,)), ((), ())), preferred_element_type=jnp.float32
    )


NEG = -1e30


def contract(first_op, second_op, first_dim, second_dim):
    return lax.dot_general(
        first_op,
        second_op,
        (((first_dim,), (second_dim,)), ((), ())),
        preferred_element_type=jnp.float32,
    )


def key_positions(shape, dim, rank, local_len):
    row = lax.broadcasted_iota(jnp.int32, shape, dim)
    return ((row // local_len) ^ rank) * local_len + row % local_len


def fwd_kernel(heads, local_len, meta_ref, q_ref, k_ref, v_ref, ctx_ref, lse_ref):
    length, rank = meta_ref[0], meta_ref[1]
    key_count = k_ref.shape[1]
    valid = key_positions((1, key_count), 1, rank, local_len) < length
    outs = []
    for h in range(heads):
        s = contract(q_ref[h], k_ref[h], 1, 1)
        s = jnp.where(valid, s, NEG)
        m = jnp.max(s, axis=1, keepdims=True)
        e = jnp.exp(s - m)
        total = jnp.sum(e, axis=1, keepdims=True)
        p = (e * (1.0 / total)).astype(jnp.bfloat16)
        outs.append(contract(p, v_ref[h], 1, 0))
        lse_ref[h] = (m + jnp.log(total)).T
    ctx_ref[...] = jnp.concatenate(outs, axis=1).astype(jnp.bfloat16)


def attend_forward(meta, q, k, v, local_len, block_rows):
    heads, key_count, _ = q.shape
    row = pl.BlockSpec((heads, block_rows, HD), lambda i, *_: (0, i, 0))
    full = pl.BlockSpec((heads, key_count, HD), lambda i, *_: (0, 0, 0))
    pairs = heads * key_count * key_count
    return pl.pallas_call(
        functools.partial(fwd_kernel, heads, local_len),
        grid_spec=pltpu.PrefetchScalarGridSpec(
            num_scalar_prefetch=1,
            grid=(key_count // block_rows,),
            in_specs=[row, full, full],
            out_specs=[
                pl.BlockSpec((block_rows, heads * HD), lambda i, *_: (i, 0)),
                pl.BlockSpec((heads, 1, block_rows), lambda i, *_: (0, 0, i)),
            ],
        ),
        out_shape=[
            jax.ShapeDtypeStruct((key_count, heads * HD), jnp.bfloat16),
            jax.ShapeDtypeStruct((heads, 1, key_count), jnp.float32),
        ],
        compiler_params=pltpu.CompilerParams(vmem_limit_bytes=48 << 20),
        cost_estimate=pl.CostEstimate(
            flops=16 * pairs * HD, bytes_accessed=8 * q.size, transcendentals=pairs
        ),
        name="attend_forward",
    )(meta, q, k, v)


def bwd_kernel(
    heads,
    local_len,
    meta_ref,
    q_ref,
    k_ref,
    v_ref,
    do_ref,
    lse_ref,
    dq_ref,
    dk_ref,
    dv_ref,
    dk_acc,
    dv_acc,
):
    length, rank = meta_ref[0], meta_ref[1]
    step = pl.program_id(0)
    key_count = k_ref.shape[1]
    valid = key_positions((key_count, 1), 0, rank, local_len) < length

    @pl.when(step == 0)
    def _():
        dk_acc[...] = jnp.zeros_like(dk_acc)
        dv_acc[...] = jnp.zeros_like(dv_acc)

    dqs = []
    for h in range(heads):
        q = q_ref[h]
        k = k_ref[h]
        do = do_ref[:, h * HD : (h + 1) * HD]
        s = jnp.where(valid, contract(k, q, 1, 1), NEG)
        p = jnp.exp(s - lse_ref[h])
        dv_acc[h] += contract(p.astype(jnp.bfloat16), do, 1, 0)
        gp = contract(v_ref[h], do, 1, 1)
        center = jnp.sum(p * gp, axis=0, keepdims=True)
        ds = (p * (gp - center)).astype(jnp.bfloat16)
        dk_acc[h] += contract(ds, q, 1, 0)
        dqs.append(contract(ds, k, 0, 0) * HD ** (-0.5))
    dq_ref[...] = jnp.concatenate(dqs, axis=1).astype(jnp.bfloat16)

    @pl.when(step == pl.num_programs(0) - 1)
    def _():
        dk_ref[...] = jnp.concatenate([dk_acc[h] for h in range(heads)], axis=1).astype(jnp.bfloat16)
        dv_ref[...] = jnp.concatenate([dv_acc[h] for h in range(heads)], axis=1).astype(jnp.bfloat16)


def attend_backward(meta, q, k, v, do, lse, local_len, block_rows):
    heads, key_count, _ = q.shape
    width = heads * HD
    row = pl.BlockSpec((heads, block_rows, HD), lambda i, *_: (0, i, 0))
    full = pl.BlockSpec((heads, key_count, HD), lambda i, *_: (0, 0, 0))
    flat = pl.BlockSpec((block_rows, width), lambda i, *_: (i, 0))
    flat_full = pl.BlockSpec((key_count, width), lambda i, *_: (0, 0))
    shape = jax.ShapeDtypeStruct((key_count, width), jnp.bfloat16)
    pairs = heads * key_count * key_count
    return pl.pallas_call(
        functools.partial(bwd_kernel, heads, local_len),
        grid_spec=pltpu.PrefetchScalarGridSpec(
            num_scalar_prefetch=1,
            grid=(key_count // block_rows,),
            in_specs=[
                row,
                full,
                full,
                flat,
                pl.BlockSpec((heads, 1, block_rows), lambda i, *_: (0, 0, i)),
            ],
            out_specs=[flat, flat_full, flat_full],
            scratch_shapes=[pltpu.VMEM((heads, key_count, HD), jnp.float32)] * 2,
        ),
        out_shape=[shape, shape, shape],
        compiler_params=pltpu.CompilerParams(vmem_limit_bytes=56 << 20),
        cost_estimate=pl.CostEstimate(
            flops=40 * pairs * HD, bytes_accessed=16 * q.size, transcendentals=pairs
        ),
        name="attend_backward",
    )(meta, q, k, v, do, lse)


def project_kernel(heads, x_ref, w_ref, b_ref, q_ref, k_ref, v_ref):
    out = contract(x_ref[...], w_ref[...], 1, 0) + b_ref[...]
    out = out.astype(jnp.bfloat16)
    for part, ref in enumerate((q_ref, k_ref, v_ref)):
        for h in range(heads):
            at = (part * heads + h) * HD
            cols = out[:, at : at + HD]
            ref[h] = cols * 0.125 if part == 0 else cols


def project(x, w, b, heads, block_rows):
    rows, width = x.shape
    out = pl.BlockSpec((heads, block_rows, HD), lambda i: (0, i, 0))
    shape = jax.ShapeDtypeStruct((heads, rows, HD), jnp.bfloat16)
    return pl.pallas_call(
        functools.partial(project_kernel, heads),
        grid=(rows // block_rows,),
        in_specs=[
            pl.BlockSpec((block_rows, width), lambda i: (i, 0)),
            pl.BlockSpec(w.shape, lambda i: (0, 0)),
            pl.BlockSpec(b.shape, lambda i: (0, 0)),
        ],
        out_specs=[out, out, out],
        out_shape=[shape, shape, shape],
        compiler_params=pltpu.CompilerParams(vmem_limit_bytes=32 << 20),
        cost_estimate=pl.CostEstimate(
            flops=2 * rows * width * w.shape[1], bytes_accessed=4 * x.size, transcendentals=0
        ),
        name="project",
    )(x, w, b)


def swap(values, bits):
    pairs = [(r, r ^ bits) for r in range(4)]
    return lax.ppermute(values, "seq", pairs)


def xor_order(values, rank, dim):
    size = values.shape[dim] // 4
    return jnp.concatenate(
        [lax.dynamic_slice_in_dim(values, (rank ^ j) * size, size, dim) for j in range(4)], axis=dim
    )


def seq_sum(values):
    low = values.astype(jnp.bfloat16)
    low = (low.astype(jnp.float32) + swap(low, 1).astype(jnp.float32)).astype(jnp.bfloat16)
    return low.astype(jnp.float32) + swap(low, 2).astype(jnp.float32)


def scatter_sum(values):
    return lax.psum_scatter(values.astype(jnp.bfloat16), "dp", scatter_dimension=0, tiled=True)


def shards(
    hidden_in,
    cotangent,
    lengths,
    qkv_weight,
    q_bias,
    v_bias,
    out_weight,
    out_bias,
    norm1_gain,
    norm1_shift,
    up_weight,
    up_bias,
    down_weight,
    down_bias,
    norm2_gain,
    norm2_shift,
):
    f32, bf16 = jnp.float32, jnp.bfloat16
    rank = lax.axis_index("seq")
    parts = lax.axis_size("dp")
    groups, local_len, width = hidden_in.shape
    own = width // 4
    heads = own // HD
    full_len = 4 * local_len
    row_count = groups * local_len
    shard = width // parts
    wide = 3 * own

    qkv_own = lax.dynamic_slice_in_dim(qkv_weight.reshape(shard, 3, width), rank * own, own, 2)
    qkv_own = qkv_own.reshape(shard, wide)
    smalls = (q_bias, v_bias, out_bias, norm1_gain, norm1_shift, down_bias, norm2_gain, norm2_shift, up_bias)
    small = jnp.concatenate(smalls)
    small_rows = -(-small.size // wide)
    small_rows += (-(shard + small_rows)) % 16
    small = jnp.pad(small, (0, small_rows * wide - small.size)).reshape(small_rows, wide)
    packed = lax.all_gather(jnp.concatenate([qkv_own, small]), "dp", axis=0, tiled=False)

    tokens = []
    for g in range(groups):
        mine = hidden_in[g]
        far = swap(mine, 2)
        both = jnp.stack([mine, far])
        near = swap(both, 1)
        tokens.append(jnp.concatenate([mine, near[0], far, near[1]], axis=0))

    w_out = lax.all_gather(out_weight, "dp", axis=0, tiled=True)
    w_up = lax.all_gather(up_weight, "dp", axis=0, tiled=True)
    w_down = lax.all_gather(down_weight, "dp", axis=0, tiled=True)

    w_own = packed[:, :shard].reshape(width, wide)
    small = packed[:, shard:].reshape(parts, small_rows * wide)
    vectors, at = [], 0
    for vec in smalls:
        vectors.append(small[:, at : at + vec.size].reshape(parts * vec.size).astype(f32))
        at += vec.size
    b_query, b_value, b_out, g_one, s_one, b_down, g_two, s_two, b_up = vectors
    bias_own = jnp.concatenate(
        [
            lax.dynamic_slice_in_dim(b_query, rank * own, own),
            jnp.zeros((own,), f32),
            lax.dynamic_slice_in_dim(b_value, rank * own, own),
        ]
    )[None]

    metas, heads_of, contexts = [], [], []
    for g in range(groups):
        meta = jnp.stack([lengths[g], rank.astype(jnp.int32)])
        q, k, v = project(tokens[g], w_own, bias_own, heads, local_len)
        ctx, lse = attend_forward(meta, q, k, v, local_len, local_len // 2)
        chunks = [ctx[j * local_len : (j + 1) * local_len] for j in range(4)]
        got = [chunks[0]] + [swap(chunks[j], j) for j in (1, 2, 3)]
        contexts.append(jnp.concatenate(got, axis=1))
        metas.append(meta)
        heads_of.append((q, k, v, lse))

    token_rows = hidden_in.reshape(row_count, width)
    ctx_rows = jnp.concatenate(contexts, axis=0)
    w_out = xor_order(w_out, rank, 0)
    attended = matmul(ctx_rows, w_out) + b_out
    first_norm, first_back = jax.vjp(norm_rows, token_rows.astype(f32) + attended, g_one, s_one)
    first_low = first_norm.astype(bf16)
    pre_act = matmul(first_low, w_up) + b_up
    activated, gelu_back = jax.vjp(gelu_exact, pre_act)
    active_low = activated.astype(bf16)
    branch = matmul(active_low, w_down) + b_down
    result, second_back = jax.vjp(norm_rows, first_norm + branch, g_two, s_two)
    grad_result = cotangent.reshape(row_count, width).astype(f32)
    grad_second, grad_g_two, grad_s_two = second_back(grad_result)
    grad_branch = grad_second.astype(bf16)
    grad_down_bias = jnp.sum(grad_branch.astype(f32), axis=0)
    sh_down = scatter_sum(inner_rows(active_low, grad_branch))
    (grad_inner,) = gelu_back(inner_cols(grad_branch, w_down))
    grad_pre = grad_inner.astype(bf16)
    grad_up_bias = jnp.sum(grad_pre.astype(f32), axis=0)
    sh_up = scatter_sum(inner_rows(first_low, grad_pre))
    grad_first = grad_second + inner_cols(grad_pre, w_up)
    grad_mid, grad_g_one, grad_s_one = first_back(grad_first)
    grad_attended = grad_mid.astype(bf16)
    grad_out_bias = jnp.sum(grad_attended.astype(f32), axis=0)
    grad_ctx = inner_cols(grad_attended, w_out).astype(bf16).reshape(groups, local_len, 4, own)
    grad_out = xor_order(inner_rows(ctx_rows, grad_attended), rank, 0)
    rest = (grad_out_bias, grad_g_one, grad_s_one, grad_down_bias, grad_g_two, grad_s_two, grad_up_bias)
    rest_all = jnp.concatenate([vec.reshape(parts, -1) for vec in rest], axis=1).astype(bf16)
    rest_rows = -(-rest_all.shape[1] // width)
    rest_rows += (-(shard + rest_rows)) % 16
    rest_all = jnp.pad(rest_all, ((0, 0), (0, rest_rows * width - rest_all.shape[1])))
    out_all = jnp.concatenate(
        [grad_out.astype(bf16).reshape(parts, shard, width), rest_all.reshape(parts, rest_rows, width)], axis=1
    )
    sh_out = scatter_sum(out_all.reshape(parts * (shard + rest_rows), width))

    grad_qkv = jnp.zeros((width, wide), f32)
    bias_sums = jnp.zeros((wide,), f32)
    grad_inputs = []
    for g in range(groups):
        q, k, v, lse = heads_of[g]
        do = [grad_ctx[g, :, 0]] + [swap(grad_ctx[g, :, j], j) for j in (1, 2, 3)]
        do = jnp.concatenate(do, axis=0)
        grads = attend_backward(metas[g], q, k, v, do, lse, local_len, local_len)
        grad_proj = jnp.concatenate(grads, axis=1)
        part = inner_cols(grad_proj, w_own).reshape(4, local_len, width)
        near = swap(part[1::2].astype(bf16), 1).astype(f32)
        far = swap((part[2] + near[1]).astype(bf16), 2).astype(f32)
        mid = grad_mid[g * local_len : (g + 1) * local_len]
        grad_inputs.append((mid + part[0] + near[0] + far).astype(bf16))
        grad_qkv = grad_qkv + inner_rows(tokens[g], grad_proj)
        bias_sums = bias_sums + jnp.sum(grad_proj.astype(f32), axis=0)

    bias_full = jnp.zeros((2, width), f32)
    bias_full = lax.dynamic_update_slice(bias_full, bias_sums[None, :own], (0, rank * own))
    bias_full = lax.dynamic_update_slice(bias_full, bias_sums[None, 2 * own :], (1, rank * own))
    bias_full = bias_full.reshape(2, parts, shard).transpose(1, 0, 2).reshape(parts, 2 * shard)
    bias_rows = -(-2 * shard // wide)
    bias_rows += (-(shard + bias_rows)) % 16
    bias_full = jnp.pad(bias_full, ((0, 0), (0, bias_rows * wide - 2 * shard)))
    qkv_all = jnp.concatenate(
        [grad_qkv.reshape(parts, shard, wide), bias_full.reshape(parts, bias_rows, wide)], axis=1
    )
    sh_qkv = scatter_sum(qkv_all.reshape(parts * (shard + bias_rows), wide))
    far = swap(sh_qkv, 2)
    both = jnp.stack([sh_qkv, far])
    near = swap(both, 1)
    four = jnp.concatenate([sh_qkv, near[0], far, near[1]], axis=0)
    four = xor_order(four, rank, 0).reshape(4, shard + bias_rows, wide).astype(f32)
    out_qkv = four[:, :shard].reshape(4, shard, 3, own).transpose(1, 2, 0, 3).reshape(shard, 3 * width)
    biases = jnp.sum(four[:, shard:].reshape(4, bias_rows * wide), axis=0)

    out_down = seq_sum(sh_down)
    out_up = seq_sum(sh_up)
    out_out = seq_sum(sh_out)
    flat = out_out[shard:].reshape(-1)
    finals, at = [], 0
    for vec in rest:
        size = vec.size // parts
        finals.append(flat[at : at + size])
        at += size
    o_bias, o_gone, o_sone, o_dbias, o_gtwo, o_stwo, o_ubias = finals
    return (
        result.astype(bf16).reshape(hidden_in.shape),
        jnp.stack(grad_inputs),
        out_qkv,
        biases[:shard],
        biases[shard : 2 * shard],
        out_out[:shard],
        o_bias,
        o_gone,
        o_sone,
        out_up,
        o_ubias,
        out_down,
        o_dbias,
        o_gtwo,
        o_stwo,
    )


def solution(mesh):
    placed = (
        P("dp", "seq", None),
        P("dp", "seq", None),
        P("dp"),
        P("dp", None),
        P("dp"),
        P("dp"),
        P("dp", None),
        P("dp"),
        P("dp"),
        P("dp"),
        P("dp", None),
        P("dp"),
        P("dp", None),
        P("dp"),
        P("dp"),
        P("dp"),
    )
    return jax.shard_map(
        shards,
        mesh=mesh,
        in_specs=placed,
        out_specs=(
            P("dp", "seq", None),
            P("dp", "seq", None),
            P("dp", None),
            P("dp"),
            P("dp"),
            P("dp", None),
            P("dp"),
            P("dp"),
            P("dp"),
            P("dp", None),
            P("dp"),
            P("dp", None),
            P("dp"),
            P("dp"),
            P("dp"),
        ),
        check_vma=False,
    )
```

```python
import functools

import jax
import jax.numpy as jnp
from jax import lax
from jax.experimental import pallas as pl
from jax.experimental.pallas import tpu as pltpu
from jax.sharding import PartitionSpec as P

HD = 64


epsilon = 1e-06


def norm_rows(values_in, gain_vec, shift_vec):
    centered = values_in - jnp.mean(values_in, axis=-1, keepdims=True)
    variance = jnp.mean(centered * centered, axis=-1, keepdims=True)
    return centered * lax.rsqrt(variance + epsilon) * gain_vec + shift_vec


def gelu_exact(values_in):
    return jax.nn.gelu(values_in, approximate=False)


def matmul(first_op, second_op):
    return jnp.dot(first_op, second_op, preferred_element_type=jnp.float32)


def inner_rows(first_op, second_op):
    return lax.dot_general(
        first_op, second_op, (((0,), (0,)), ((), ())), preferred_element_type=jnp.float32
    )


def inner_cols(first_op, second_op):
    return lax.dot_general(
        first_op, second_op, (((1,), (1,)), ((), ())), preferred_element_type=jnp.float32
    )


NEG = -1e30


def contract(first_op, second_op, first_dim, second_dim):
    return lax.dot_general(
        first_op,
        second_op,
        (((first_dim,), (second_dim,)), ((), ())),
        preferred_element_type=jnp.float32,
    )


def key_positions(shape, dim, rank, local_len):
    row = lax.broadcasted_iota(jnp.int32, shape, dim)
    return ((row // local_len) ^ rank) * local_len + row % local_len


def fwd_kernel(heads, local_len, meta_ref, q_ref, k_ref, v_ref, ctx_ref, lse_ref):
    length, rank = meta_ref[0], meta_ref[1]
    key_count = k_ref.shape[1]
    valid = key_positions((1, key_count), 1, rank, local_len) < length
    outs = []
    for h in range(heads):
        s = contract(q_ref[h], k_ref[h], 1, 1)
        s = jnp.where(valid, s, NEG)
        m = jnp.max(s, axis=1, keepdims=True)
        e = jnp.exp(s - m)
        total = jnp.sum(e, axis=1, keepdims=True)
        p = (e * (1.0 / total)).astype(jnp.bfloat16)
        outs.append(contract(p, v_ref[h], 1, 0))
        lse_ref[h] = (m + jnp.log(total)).T
    ctx_ref[...] = jnp.concatenate(outs, axis=1).astype(jnp.bfloat16)


def attend_forward(meta, q, k, v, local_len, block_rows):
    heads, key_count, _ = q.shape
    row = pl.BlockSpec((heads, block_rows, HD), lambda i, *_: (0, i, 0))
    full = pl.BlockSpec((heads, key_count, HD), lambda i, *_: (0, 0, 0))
    pairs = heads * key_count * key_count
    return pl.pallas_call(
        functools.partial(fwd_kernel, heads, local_len),
        grid_spec=pltpu.PrefetchScalarGridSpec(
            num_scalar_prefetch=1,
            grid=(key_count // block_rows,),
            in_specs=[row, full, full],
            out_specs=[
                pl.BlockSpec((block_rows, heads * HD), lambda i, *_: (i, 0)),
                pl.BlockSpec((heads, 1, block_rows), lambda i, *_: (0, 0, i)),
            ],
        ),
        out_shape=[
            jax.ShapeDtypeStruct((key_count, heads * HD), jnp.bfloat16),
            jax.ShapeDtypeStruct((heads, 1, key_count), jnp.float32),
        ],
        compiler_params=pltpu.CompilerParams(vmem_limit_bytes=48 << 20),
        cost_estimate=pl.CostEstimate(
            flops=16 * pairs * HD, bytes_accessed=8 * q.size, transcendentals=pairs
        ),
        name="attend_forward",
    )(meta, q, k, v)


def bwd_kernel(
    heads,
    local_len,
    meta_ref,
    q_ref,
    k_ref,
    v_ref,
    do_ref,
    lse_ref,
    dq_ref,
    dk_ref,
    dv_ref,
    dk_acc,
    dv_acc,
):
    length, rank = meta_ref[0], meta_ref[1]
    step = pl.program_id(0)
    key_count = k_ref.shape[1]
    valid = key_positions((key_count, 1), 0, rank, local_len) < length

    @pl.when(step == 0)
    def _():
        dk_acc[...] = jnp.zeros_like(dk_acc)
        dv_acc[...] = jnp.zeros_like(dv_acc)

    dqs = []
    for h in range(heads):
        q = q_ref[h]
        k = k_ref[h]
        do = do_ref[:, h * HD : (h + 1) * HD]
        s = jnp.where(valid, contract(k, q, 1, 1), NEG)
        p = jnp.exp(s - lse_ref[h])
        dv_acc[h] += contract(p.astype(jnp.bfloat16), do, 1, 0)
        gp = contract(v_ref[h], do, 1, 1)
        center = jnp.sum(p * gp, axis=0, keepdims=True)
        ds = (p * (gp - center)).astype(jnp.bfloat16)
        dk_acc[h] += contract(ds, q, 1, 0)
        dqs.append(contract(ds, k, 0, 0) * HD ** (-0.5))
    dq_ref[...] = jnp.concatenate(dqs, axis=1).astype(jnp.bfloat16)

    @pl.when(step == pl.num_programs(0) - 1)
    def _():
        dk_ref[...] = jnp.concatenate([dk_acc[h] for h in range(heads)], axis=1).astype(jnp.bfloat16)
        dv_ref[...] = jnp.concatenate([dv_acc[h] for h in range(heads)], axis=1).astype(jnp.bfloat16)


def attend_backward(meta, q, k, v, do, lse, local_len, block_rows):
    heads, key_count, _ = q.shape
    width = heads * HD
    row = pl.BlockSpec((heads, block_rows, HD), lambda i, *_: (0, i, 0))
    full = pl.BlockSpec((heads, key_count, HD), lambda i, *_: (0, 0, 0))
    flat = pl.BlockSpec((block_rows, width), lambda i, *_: (i, 0))
    flat_full = pl.BlockSpec((key_count, width), lambda i, *_: (0, 0))
    shape = jax.ShapeDtypeStruct((key_count, width), jnp.bfloat16)
    pairs = heads * key_count * key_count
    return pl.pallas_call(
        functools.partial(bwd_kernel, heads, local_len),
        grid_spec=pltpu.PrefetchScalarGridSpec(
            num_scalar_prefetch=1,
            grid=(key_count // block_rows,),
            in_specs=[
                row,
                full,
                full,
                flat,
                pl.BlockSpec((heads, 1, block_rows), lambda i, *_: (0, 0, i)),
            ],
            out_specs=[flat, flat_full, flat_full],
            scratch_shapes=[pltpu.VMEM((heads, key_count, HD), jnp.float32)] * 2,
        ),
        out_shape=[shape, shape, shape],
        compiler_params=pltpu.CompilerParams(vmem_limit_bytes=56 << 20),
        cost_estimate=pl.CostEstimate(
            flops=40 * pairs * HD, bytes_accessed=16 * q.size, transcendentals=pairs
        ),
        name="attend_backward",
    )(meta, q, k, v, do, lse)


def project_kernel(heads, x_ref, w_ref, b_ref, q_ref, k_ref, v_ref):
    out = contract(x_ref[...], w_ref[...], 1, 0) + b_ref[...]
    out = out.astype(jnp.bfloat16)
    for part, ref in enumerate((q_ref, k_ref, v_ref)):
        for h in range(heads):
            at = (part * heads + h) * HD
            cols = out[:, at : at + HD]
            ref[h] = cols * 0.125 if part == 0 else cols


def project(x, w, b, heads, block_rows):
    rows, width = x.shape
    out = pl.BlockSpec((heads, block_rows, HD), lambda i: (0, i, 0))
    shape = jax.ShapeDtypeStruct((heads, rows, HD), jnp.bfloat16)
    return pl.pallas_call(
        functools.partial(project_kernel, heads),
        grid=(rows // block_rows,),
        in_specs=[
            pl.BlockSpec((block_rows, width), lambda i: (i, 0)),
            pl.BlockSpec(w.shape, lambda i: (0, 0)),
            pl.BlockSpec(b.shape, lambda i: (0, 0)),
        ],
        out_specs=[out, out, out],
        out_shape=[shape, shape, shape],
        compiler_params=pltpu.CompilerParams(vmem_limit_bytes=32 << 20),
        cost_estimate=pl.CostEstimate(
            flops=2 * rows * width * w.shape[1], bytes_accessed=4 * x.size, transcendentals=0
        ),
        name="project",
    )(x, w, b)


def swap(values, bits):
    pairs = [(r, r ^ bits) for r in range(4)]
    return lax.ppermute(values, "seq", pairs)


def xor_order(values, rank, dim):
    size = values.shape[dim] // 4
    return jnp.concatenate(
        [lax.dynamic_slice_in_dim(values, (rank ^ j) * size, size, dim) for j in range(4)], axis=dim
    )


def seq_sum(values):
    low = values.astype(jnp.bfloat16)
    low = (low.astype(jnp.float32) + swap(low, 1).astype(jnp.float32)).astype(jnp.bfloat16)
    return low.astype(jnp.float32) + swap(low, 2).astype(jnp.float32)


def scatter_sum(values):
    return lax.psum_scatter(values.astype(jnp.bfloat16), "dp", scatter_dimension=0, tiled=True)


def shards(
    hidden_in,
    cotangent,
    lengths,
    qkv_weight,
    q_bias,
    v_bias,
    out_weight,
    out_bias,
    norm1_gain,
    norm1_shift,
    up_weight,
    up_bias,
    down_weight,
    down_bias,
    norm2_gain,
    norm2_shift,
):
    f32, bf16 = jnp.float32, jnp.bfloat16
    rank = lax.axis_index("seq")
    parts = lax.axis_size("dp")
    groups, local_len, width = hidden_in.shape
    own = width // 4
    heads = own // HD
    full_len = 4 * local_len
    row_count = groups * local_len
    shard = width // parts
    wide = 3 * own

    qkv_own = lax.dynamic_slice_in_dim(qkv_weight.reshape(shard, 3, width), rank * own, own, 2)
    qkv_own = qkv_own.reshape(shard, wide)
    smalls = (q_bias, v_bias, out_bias, norm1_gain, norm1_shift, down_bias, norm2_gain, norm2_shift, up_bias)
    small = jnp.concatenate(smalls)
    small_rows = -(-small.size // wide)
    small_rows += (-(shard + small_rows)) % 16
    small = jnp.pad(small, (0, small_rows * wide - small.size)).reshape(small_rows, wide)
    packed = lax.all_gather(jnp.concatenate([qkv_own, small]), "dp", axis=0, tiled=False)

    tokens = []
    for g in range(groups):
        mine = hidden_in[g]
        far = swap(mine, 2)
        both = jnp.stack([mine, far])
        near = swap(both, 1)
        tokens.append(jnp.concatenate([mine, near[0], far, near[1]], axis=0))

    w_out = lax.all_gather(out_weight, "dp", axis=0, tiled=True)
    w_up = lax.all_gather(up_weight, "dp", axis=0, tiled=True)
    w_down = lax.all_gather(down_weight, "dp", axis=0, tiled=True)

    w_own = packed[:, :shard].reshape(width, wide)
    small = packed[:, shard:].reshape(parts, small_rows * wide)
    vectors, at = [], 0
    for vec in smalls:
        vectors.append(small[:, at : at + vec.size].reshape(parts * vec.size).astype(f32))
        at += vec.size
    b_query, b_value, b_out, g_one, s_one, b_down, g_two, s_two, b_up = vectors
    bias_own = jnp.concatenate(
        [
            lax.dynamic_slice_in_dim(b_query, rank * own, own),
            jnp.zeros((own,), f32),
            lax.dynamic_slice_in_dim(b_value, rank * own, own),
        ]
    )[None]

    metas, heads_of, contexts = [], [], []
    for g in range(groups):
        meta = jnp.stack([lengths[g], rank.astype(jnp.int32)])
        q, k, v = project(tokens[g], w_own, bias_own, heads, local_len)
        ctx, lse = attend_forward(meta, q, k, v, local_len, local_len // 2)
        chunks = [ctx[j * local_len : (j + 1) * local_len] for j in range(4)]
        got = [chunks[0]] + [swap(chunks[j], j) for j in (1, 2, 3)]
        contexts.append(jnp.concatenate(got, axis=1))
        metas.append(meta)
        heads_of.append((q, k, v, lse))

    token_rows = hidden_in.reshape(row_count, width)
    ctx_rows = jnp.concatenate(contexts, axis=0)
    w_out = xor_order(w_out, rank, 0)
    attended = matmul(ctx_rows, w_out) + b_out
    first_norm, first_back = jax.vjp(norm_rows, token_rows.astype(f32) + attended, g_one, s_one)
    first_low = first_norm.astype(bf16)
    pre_act = matmul(first_low, w_up) + b_up
    activated, gelu_back = jax.vjp(gelu_exact, pre_act)
    active_low = activated.astype(bf16)
    branch = matmul(active_low, w_down) + b_down
    result, second_back = jax.vjp(norm_rows, first_norm + branch, g_two, s_two)
    grad_result = cotangent.reshape(row_count, width).astype(f32)
    grad_second, grad_g_two, grad_s_two = second_back(grad_result)
    grad_branch = grad_second.astype(bf16)
    grad_down_bias = jnp.sum(grad_branch.astype(f32), axis=0)
    grad_down = inner_rows(active_low, grad_branch).astype(bf16)
    (grad_inner,) = gelu_back(inner_cols(grad_branch, w_down))
    grad_pre = grad_inner.astype(bf16)
    grad_up_bias = jnp.sum(grad_pre.astype(f32), axis=0)
    grad_up = inner_rows(first_low, grad_pre).astype(bf16)
    grad_first = grad_second + inner_cols(grad_pre, w_up)
    grad_mid, grad_g_one, grad_s_one = first_back(grad_first)
    grad_attended = grad_mid.astype(bf16)
    grad_out_bias = jnp.sum(grad_attended.astype(f32), axis=0)
    grad_ctx = inner_cols(grad_attended, w_out).astype(bf16).reshape(groups, local_len, 4, own)
    grad_out = xor_order(inner_rows(ctx_rows, grad_attended), rank, 0)
    rest = (grad_out_bias, grad_g_one, grad_s_one, grad_down_bias, grad_g_two, grad_s_two, grad_up_bias)
    rest_all = jnp.concatenate([vec.reshape(parts, -1) for vec in rest], axis=1).astype(bf16)
    rest_rows = -(-rest_all.shape[1] // width)
    rest_rows += (-(shard + rest_rows)) % 16
    rest_all = jnp.pad(rest_all, ((0, 0), (0, rest_rows * width - rest_all.shape[1])))
    out_all = jnp.concatenate(
        [grad_out.astype(bf16).reshape(parts, shard, width), rest_all.reshape(parts, rest_rows, width)], axis=1
    )
    out_all = out_all.reshape(parts * (shard + rest_rows), width)
    grad_down, grad_up, out_all, grad_ctx = lax.optimization_barrier(
        (grad_down, grad_up, out_all, grad_ctx)
    )
    sh_down = scatter_sum(grad_down)
    sh_up = scatter_sum(grad_up)
    sh_out = scatter_sum(out_all)

    grad_qkv = jnp.zeros((width, wide), f32)
    bias_sums = jnp.zeros((wide,), f32)
    grad_inputs = []
    for g in range(groups):
        q, k, v, lse = heads_of[g]
        do = [grad_ctx[g, :, 0]] + [swap(grad_ctx[g, :, j], j) for j in (1, 2, 3)]
        do = jnp.concatenate(do, axis=0)
        grads = attend_backward(metas[g], q, k, v, do, lse, local_len, local_len)
        grad_proj = jnp.concatenate(grads, axis=1)
        part = inner_cols(grad_proj, w_own).reshape(4, local_len, width)
        near = swap(part[1::2].astype(bf16), 1).astype(f32)
        far = swap((part[2] + near[1]).astype(bf16), 2).astype(f32)
        mid = grad_mid[g * local_len : (g + 1) * local_len]
        grad_inputs.append((mid + part[0] + near[0] + far).astype(bf16))
        grad_qkv = grad_qkv + inner_rows(tokens[g], grad_proj)
        bias_sums = bias_sums + jnp.sum(grad_proj.astype(f32), axis=0)

    bias_full = jnp.zeros((2, width), f32)
    bias_full = lax.dynamic_update_slice(bias_full, bias_sums[None, :own], (0, rank * own))
    bias_full = lax.dynamic_update_slice(bias_full, bias_sums[None, 2 * own :], (1, rank * own))
    bias_full = bias_full.reshape(2, parts, shard).transpose(1, 0, 2).reshape(parts, 2 * shard)
    bias_rows = -(-2 * shard // wide)
    bias_rows += (-(shard + bias_rows)) % 16
    bias_full = jnp.pad(bias_full, ((0, 0), (0, bias_rows * wide - 2 * shard)))
    qkv_all = jnp.concatenate(
        [grad_qkv.reshape(parts, shard, wide), bias_full.reshape(parts, bias_rows, wide)], axis=1
    )
    qkv_all, sh_down, sh_up, sh_out = lax.optimization_barrier((qkv_all, sh_down, sh_up, sh_out))
    sh_qkv = scatter_sum(qkv_all.reshape(parts * (shard + bias_rows), wide))
    far = swap(sh_qkv, 2)
    both = jnp.stack([sh_qkv, far])
    near = swap(both, 1)
    four = jnp.concatenate([sh_qkv, near[0], far, near[1]], axis=0)
    four = xor_order(four, rank, 0).reshape(4, shard + bias_rows, wide).astype(f32)
    out_qkv = four[:, :shard].reshape(4, shard, 3, own).transpose(1, 2, 0, 3).reshape(shard, 3 * width)
    biases = jnp.sum(four[:, shard:].reshape(4, bias_rows * wide), axis=0)

    out_down = seq_sum(sh_down)
    out_up = seq_sum(sh_up)
    out_out = seq_sum(sh_out)
    flat = out_out[shard:].reshape(-1)
    finals, at = [], 0
    for vec in rest:
        size = vec.size // parts
        finals.append(flat[at : at + size])
        at += size
    o_bias, o_gone, o_sone, o_dbias, o_gtwo, o_stwo, o_ubias = finals
    return (
        result.astype(bf16).reshape(hidden_in.shape),
        jnp.stack(grad_inputs),
        out_qkv,
        biases[:shard],
        biases[shard : 2 * shard],
        out_out[:shard],
        o_bias,
        o_gone,
        o_sone,
        out_up,
        o_ubias,
        out_down,
        o_dbias,
        o_gtwo,
        o_stwo,
    )


def solution(mesh):
    placed = (
        P("dp", "seq", None),
        P("dp", "seq", None),
        P("dp"),
        P("dp", None),
        P("dp"),
        P("dp"),
        P("dp", None),
        P("dp"),
        P("dp"),
        P("dp"),
        P("dp", None),
        P("dp"),
        P("dp", None),
        P("dp"),
        P("dp"),
        P("dp"),
    )
    return jax.shard_map(
        shards,
        mesh=mesh,
        in_specs=placed,
        out_specs=(
            P("dp", "seq", None),
            P("dp", "seq", None),
            P("dp", None),
            P("dp"),
            P("dp"),
            P("dp", None),
            P("dp"),
            P("dp"),
            P("dp"),
            P("dp", None),
            P("dp"),
            P("dp", None),
            P("dp"),
            P("dp"),
            P("dp"),
        ),
        check_vma=False,
    )
```
